256 devices in a mesh: dp: 4 (over z_lo), tile: 64 (over z_hi, x, y, core).
Axes of the slice: x: 4, y: 4, z: 8 (z_hi: 2, z_lo: 4; z = z_hi * 4 + z_lo), core: 2. Of those that a mesh axis runs over, the one named last changes fastest.
Arguments:
- query: bfloat16 [4, 24576, 1536], P('dp', 'tile'), may hold values from -6 to 6
- key: bfloat16 [4, 24576, 1536], P('dp', 'tile'), may hold values from -6 to 6
- value: bfloat16 [4, 24576, 1536], P('dp', 'tile'), may hold values from -6 to 6
- text_key: bfloat16 [4, 128, 1536], P('dp', 'tile'), may hold values from -6 to 6
- text_value: bfloat16 [4, 128, 1536], P('dp', 'tile'), may hold values from -6 to 6
- text_len: int32 [4], P('dp'), may hold values from 17 to 128
- window: int32 [4, 64, 2], P('dp'), may hold values 0 or 1
- query_gain: float32 [128], replicated, may hold values from 0.5 to 3
- key_gain: float32 [128], replicated, may hold values from 0.5 to 3
- grad_out: bfloat16 [4, 24576, 1536], P('dp', 'tile'), may hold values from -6 to 6
Outputs:
- attended: bfloat16 [4, 24576, 1536], P('dp', 'tile')
- grad_query: bfloat16 [4, 24576, 1536], P('dp', 'tile')
- grad_key: bfloat16 [4, 24576, 1536], P('dp', 'tile')
- grad_value: bfloat16 [4, 24576, 1536], P('dp', 'tile')
- grad_text_key: float32 [4, 128, 1536], P('dp', 'tile')
- grad_text_value: float32 [4, 128, 1536], P('dp', 'tile')
- grad_query_gain: float32 [128], replicated
- grad_key_gain: float32 [128], replicated
The draws below stay inside these ranges and needn't reach their ends.
All inputs are finite; a program needn't handle non-finite values. No bound on the sum of `window` on one device may be relied on, other than what follows from the above.
Results may differ from the reference program's by a relative error of at most 0.012.
The reference program's roundings to bfloat16 on the way count: a program that leaves them out, or rounds other values in their place, can miss the bound.
Values may be sent and summed in bfloat16 or wider, within the bound.
No kernel may reach another device: no remote copies, remote signals or barrier semaphores. Data moves between devices by JAX's collectives and lax.ppermute only.
A program may use at most 128 MiB of HBM per device.

```python
import math
import jax
import jax.numpy as jnp
from jax import lax

HEADS = 12
HEAD = 128
TT = 384
W = 1536
TILES = 64
SEQ = 24576
TXT = 128
CLIPS = 4


def set_ends(result, own_key, smallest, high):
    place = [jax.random.randint(jax.random.fold_in(own_key, axis), (), 0, length) for axis, length in enumerate(result.shape)]
    widest = result.shape.index(max(result.shape))
    neighbour = place[:widest] + [(place[widest] + 1) % result.shape[widest]] + place[widest + 1:]
    return result.at[tuple(place)].set(smallest).at[tuple(neighbour)].set(high)


def block_levels(rng, shape, cuts, smallest, largest):
    def one(dim, blocks):
        steps = jax.random.uniform(jax.random.fold_in(jax.random.fold_in(rng, 6), dim), (blocks,), jnp.float32, smallest / len(cuts), largest / len(cuts))
        return jnp.repeat(jnp.exp(steps), shape[dim] // blocks).reshape((-1,) + (1,) * (len(shape) - dim - 1))

    factor_of = one(*cuts[0])
    for cut in cuts[1:]:
        factor_of = factor_of * one(*cut)
    return factor_of


def noise(rng, dims, scale, limit, split=(), dtype=jnp.bfloat16):
    drawn = jax.random.normal(rng, dims, jnp.float32) * scale
    if len(split) > 0:
        drawn = block_levels(rng, dims, split, -0.22, 0.18) * drawn
    return jnp.clip(drawn, min=-limit, max=limit).astype(dtype)


def setup_inputs(seed: int = 0) -> dict:
    seeds = jax.random.split(jax.random.key(seed), 11)
    query = noise(seeds[0], (CLIPS, SEQ, W), 1.0, 6.0, ((0, 4), (1, 64)))
    key = noise(seeds[1], (CLIPS, SEQ, W), 1.0, 6.0, ((0, 4), (1, 64)))
    value = noise(seeds[2], (CLIPS, SEQ, W), 1.0, 6.0, ((0, 4), (1, 64)))
    text_key = noise(seeds[3], (CLIPS, TXT, W), 1.0, 6.0, ((0, 4), (1, 64)))
    text_value = noise(seeds[4], (CLIPS, TXT, W), 1.0, 6.0, ((0, 4), (1, 64)))
    text_len = set_ends(jax.random.randint(seeds[5], (CLIPS,), TXT // 8 + 1, TXT + 1), jax.random.fold_in(seeds[5], 1), TXT // 8 + 1, TXT).astype(jnp.int32)
    window = set_ends((jax.random.randint(seeds[6], (CLIPS, TILES, 2), 0, 4) < 3).astype(jnp.int32), jax.random.fold_in(seeds[6], 1), 0, 1)
    query_gain = jnp.clip(jnp.exp(jax.random.uniform(seeds[7], (HEAD,), jnp.float32, math.log(0.5), math.log(3.0))), 0.5, 3.0)
    key_gain = jnp.clip(jnp.exp(jax.random.uniform(seeds[8], (HEAD,), jnp.float32, math.log(0.5), math.log(3.0))), 0.5, 3.0)
    grad_out = noise(seeds[9], (CLIPS, SEQ, W), 1.0, 6.0, ((0, 4), (1, 64)))
    return {"query": query, "key": key, "value": value, "text_key": text_key, "text_value": text_value, "text_len": text_len, "window": window, "query_gain": query_gain, "key_gain": key_gain, "grad_out": grad_out}


def normed(x, gain):
    count = x.shape[0]
    values = x.astype(jnp.float32).reshape(count, HEADS, HEAD)
    inverse = lax.rsqrt(lax.optimization_barrier(jnp.mean(values * values, -1, keepdims=True)) + 1e-06)
    return ((values * inverse * gain).astype(jnp.bfloat16).reshape(count, -1), values, inverse)

def norm_back(values, inverse, gain, grad):
    count = values.shape[0]
    grad = grad.reshape(count, HEADS, HEAD)
    scaled = grad * gain
    dx = inverse * scaled - values * inverse ** 3 * lax.optimization_barrier(jnp.mean(scaled * values, -1, keepdims=True))
    return (dx.reshape(count, -1), lax.optimization_barrier(jnp.sum(grad * values * inverse, (0, 1))))

def heads_first(x):
    return x.reshape(x.shape[0], HEADS, HEAD).transpose(1, 0, 2)

def heads_last(x):
    return x.transpose(1, 0, 2).reshape(x.shape[1], -1)

def head_forward(qh, kh, vh, keep):
    scale = HEAD ** (-0.5)
    scores = jnp.dot(qh.astype(jnp.float32), kh.astype(jnp.float32).T) * scale
    scores = jnp.where(keep[None, :], scores, -1e+30)
    top = lax.optimization_barrier(jnp.max(scores, -1, keepdims=True))
    expo = jnp.exp(scores - top)
    total = lax.optimization_barrier(jnp.sum(expo, -1, keepdims=True))
    probs = (expo / total).astype(jnp.bfloat16)
    out = jnp.dot(probs.astype(jnp.float32), vh.astype(jnp.float32))
    return (out, top[:, 0] + jnp.log(total[:, 0]))

def head_grads(qh, kh, vh, doh, lse, delta, keep):
    scale = HEAD ** (-0.5)
    scores = jnp.dot(qh.astype(jnp.float32), kh.astype(jnp.float32).T) * scale
    scores = jnp.where(keep[None, :], scores, -1e+30)
    pfull = jnp.exp(scores - lse[:, None])
    probs = pfull.astype(jnp.bfloat16)
    dprob = jnp.dot(doh.astype(jnp.float32), vh.astype(jnp.float32).T)
    dscore = (pfull * (dprob - delta[:, None]) * scale).astype(jnp.bfloat16).astype(jnp.float32)
    dq = jnp.dot(dscore, kh.astype(jnp.float32))
    dk = jnp.dot(dscore.T, qh.astype(jnp.float32))
    dv = jnp.dot(probs.astype(jnp.float32).T, doh.astype(jnp.float32))
    return (dq, dk, dv)

def one_clip(query, key, value, text_key, text_value, text_len, window, query_gain, key_gain, grad_out):
    qn, qvals, qinv = normed(query, query_gain)
    kn, kvals, kinv = normed(key, key_gain)
    tn, tvals, tinv = normed(text_key, key_gain)
    width = qn.shape[1]
    qt = qn.reshape(TILES, TT, width)
    gt = grad_out.reshape(TILES, TT, width)
    pad_k = jnp.pad(kn.reshape(TILES, TT, width), ((1, 1), (0, 0), (0, 0)))
    pad_v = jnp.pad(value.reshape(TILES, TT, width), ((1, 1), (0, 0), (0, 0)))
    tile_ids = jnp.arange(TILES)
    left_ok = (window[:, 0] > 0) & (tile_ids > 0)
    right_ok = (window[:, 1] > 0) & (tile_ids < TILES - 1)
    text_ok = jnp.arange(TXT) < text_len
    own = jnp.ones((TT,), bool)

    def per_tile(index):
        keys = jnp.concatenate([pad_k[index], pad_k[index + 1], pad_k[index + 2], tn], 0)
        vals = jnp.concatenate([pad_v[index], pad_v[index + 1], pad_v[index + 2], text_value], 0)
        keep = jnp.concatenate([jnp.broadcast_to(left_ok[index], (TT,)), own, jnp.broadcast_to(right_ok[index], (TT,)), text_ok])
        qh, kh, vh, doh = (heads_first(qt[index]), heads_first(keys), heads_first(vals), heads_first(gt[index]))
        out, lse = lax.map(lambda a: head_forward(a[0], a[1], a[2], keep), (qh, kh, vh))
        attended = heads_last(out).astype(jnp.bfloat16)
        delta = lax.optimization_barrier(jnp.sum(doh.astype(jnp.float32) * heads_first(attended).astype(jnp.float32), -1))
        dq, dk, dv = lax.map(lambda a: head_grads(a[0], a[1], a[2], a[3], a[4], a[5], keep), (qh, kh, vh, doh, lse, delta))
        return (attended, heads_last(dq), heads_last(dk), heads_last(dv))
    attended, dqn, dk_all, dv_all = lax.map(per_tile, jnp.arange(TILES))
    zero = jnp.zeros((1, TT, width), jnp.float32)

    def collect(all_grads):
        mid = all_grads[:, TT:2 * TT]
        from_upper = jnp.concatenate([all_grads[1:, :TT], zero], 0)
        from_lower = jnp.concatenate([zero, all_grads[:-1, 2 * TT:3 * TT]], 0)
        return ((mid + from_upper + from_lower).reshape(SEQ, width), lax.optimization_barrier(jnp.sum(all_grads[:, 3 * TT:], 0)))
    dkn, dtn = collect(dk_all)
    dv, dtv = collect(dv_all)
    grad_query, gain_q = norm_back(qvals, qinv, query_gain, dqn.reshape(SEQ, width))
    grad_key, gain_k = norm_back(kvals, kinv, key_gain, dkn)
    grad_text_key, gain_t = norm_back(tvals, tinv, key_gain, dtn)
    return (attended.reshape(SEQ, width), grad_query.astype(jnp.bfloat16), grad_key.astype(jnp.bfloat16), dv.astype(jnp.bfloat16), grad_text_key, dtv, gain_q, gain_k + gain_t)

def reference(query, key, value, text_key, text_value, text_len, window, query_gain, key_gain, grad_out):
    results = lax.map(lambda a: one_clip(a[0], a[1], a[2], a[3], a[4], a[5], a[6], query_gain, key_gain, a[7]), (query, key, value, text_key, text_value, text_len, window, grad_out))
    return (results[0], results[1], results[2], results[3], results[4], results[5], lax.optimization_barrier(jnp.sum(results[6], 0)), lax.optimization_barrier(jnp.sum(results[7], 0)))
```

```python
import functools
import math

import jax
import jax.numpy as jnp
from jax import lax
from jax.experimental import pallas as pl
from jax.experimental.pallas import tpu as pltpu
from jax.sharding import PartitionSpec as P

HEADS = 12
HEAD = 128
TT = 384
TXT = 128
W = HEADS * HEAD
CHUNKS = 2
PER = HEADS // CHUNKS
CW = PER * HEAD
SCALE = HEAD ** (-0.5)
BIG = 1e30
F32 = jnp.float32
BF16 = jnp.bfloat16

SIZES = (2, 4, 4, 2)


def place_of(zh, x, y, c):
    return ((zh * 4 + x) * 4 + y) * 2 + c


def steps_along(dim, by):
    pairs = []
    for i in range(64):
        at = [i // 32, i // 8 % 4, i // 2 % 4, i % 2]
        to = list(at)
        to[dim] = (at[dim] + by) % SIZES[dim]
        pairs.append((i, place_of(*to)))
    return pairs


def nt(a, b):
    return lax.dot_general(a, b, (((1,), (1,)), ((), ())), preferred_element_type=F32)


def nn(a, b):
    return lax.dot_general(a, b, (((1,), (0,)), ((), ())), preferred_element_type=F32)


def normed(x, gain):
    x = x.astype(F32)
    inv = lax.rsqrt(jnp.mean(x * x, -1, keepdims=True) + 1e-06)
    hat = x * inv
    return x, inv, hat, (hat * gain).astype(BF16)


def attend_kernel(flags, q_ref, k_ref, v_ref, g_ref, lo_ref, hi_ref, t_ref, keep_ref, qg_ref, kg_ref, *rest):
    att_ref, gq_ref, own_ref, dlo_ref, dhi_ref, dt_ref, gain_ref, s_ref, p_ref, d_ref = rest[-10:]
    step = pl.program_id(0)
    qg, kg = qg_ref[...], kg_ref[...]
    q, q_inv, q_hat, qn = normed(q_ref[...], qg)
    scaled = qn.astype(F32) * (SCALE * math.log2(math.e))
    high = scaled.astype(BF16)
    low = (scaled - high.astype(F32)).astype(BF16)
    queries = jnp.concatenate([high, low], 1)
    lower, upper = flags[0] > 0, flags[1] > 0

    raw = (lo_ref[0], k_ref[...], hi_ref[0], t_ref[0])
    vals = (lo_ref[1], v_ref[...], hi_ref[1], t_ref[1])
    starts = (0, TT, 2 * TT, 3 * TT)
    rows = (TT, TT, TT, TXT)
    hats, keys = [], []
    for x in raw:
        _, _, hat, kn = normed(x, kg)
        hats.append(hat)
        keys.append(kn)

    tops = []
    for b in range(4):
        s = nt(jnp.concatenate([keys[b], keys[b]], 1), queries)
        if b == 3:
            s = jnp.where(keep_ref[...] > 0, s, -BIG)
        s_ref[pl.ds(starts[b], rows[b]), :] = s
        top = jnp.max(s, 0, keepdims=True)
        if b == 0:
            top = jnp.where(lower, top, -BIG)
        if b == 2:
            top = jnp.where(upper, top, -BIG)
        tops.append(top)
    top = jnp.maximum(jnp.maximum(tops[0], tops[1]), jnp.maximum(tops[2], tops[3]))
    total = jnp.zeros((1, TT), F32)
    for b in range(4):
        shift = top
        if b == 0:
            shift = jnp.where(lower, top, BIG)
        if b == 2:
            shift = jnp.where(upper, top, BIG)
        e = jnp.exp2(s_ref[pl.ds(starts[b], rows[b]), :] - shift)
        s_ref[pl.ds(starts[b], rows[b]), :] = e
        total += jnp.sum(e, 0, keepdims=True)
    part = 1.0 / total
    out = jnp.zeros((HEAD, TT), F32)
    for b in range(4):
        p = s_ref[pl.ds(starts[b], rows[b]), :] * part
        s_ref[pl.ds(starts[b], rows[b]), :] = p
        p16 = p.astype(BF16)
        p_ref[pl.ds(starts[b], rows[b]), :] = p16
        out += nn(vals[b].T, p16)
    att = out.T.astype(BF16)
    att_ref[...] = att

    g = g_ref[...]
    delta = jnp.sum(g.astype(F32) * att.astype(F32), -1, keepdims=True)
    lane = lax.broadcasted_iota(jnp.int32, (TT, HEAD), 1)
    d1 = delta.astype(BF16).astype(F32)
    d2 = (delta - d1).astype(BF16).astype(F32)
    d3 = delta - d1 - d2
    extra = jnp.where(lane == 0, -d1, jnp.where(lane == 1, -d2, jnp.where(lane == 2, -d3, 0.0)))
    cot = jnp.concatenate([g, extra.astype(BF16)], 1)
    dq = jnp.zeros((HEAD, TT), F32)
    gain_k = jnp.zeros((1, HEAD), F32)
    for b in range(4):
        ones = (lax.broadcasted_iota(jnp.int32, (rows[b], HEAD), 1) < 3).astype(F32).astype(BF16)
        dp = nt(jnp.concatenate([vals[b], ones], 1), cot)
        ds = (s_ref[pl.ds(starts[b], rows[b]), :] * dp).astype(BF16)
        d_ref[pl.ds(starts[b], rows[b]), :] = ds
        dq += nn(keys[b].T, ds)
        dk = nn(ds, qn) * SCALE
        dv = nn(p_ref[pl.ds(starts[b], rows[b]), :], g)
        gain_k += jnp.sum(dk * hats[b], 0, keepdims=True)
        into = (dlo_ref, own_ref, dhi_ref, dt_ref)[b]
        into[0] = dk.astype(into.dtype)
        into[1] = dv.astype(into.dtype)
    dqn = dq.T * SCALE
    u = dqn * qg
    gq_ref[...] = (q_inv * u - q_hat * (q_inv * q_inv) * jnp.mean(u * q, -1, keepdims=True)).astype(BF16)
    gain_q = jnp.sum(dqn * q_hat, 0, keepdims=True)
    row = lax.broadcasted_iota(jnp.int32, (8, HEAD), 0)
    gains = jnp.where(row == 0, gain_q, jnp.where(row == 1, gain_k, 0.0))

    @pl.when(step == 0)
    def _():
        gain_ref[...] = gains

    @pl.when(step > 0)
    def _():
        gain_ref[...] += gains


def attend(chunk, flags, q, k, v, g, lo, hi, text, keep, qg, kg, before):
    base = chunk * PER
    wide = pl.BlockSpec((TT, HEAD), lambda h, f: (0, h + base))
    pair = pl.BlockSpec((2, TT, HEAD), lambda h, f: (0, 0, h))
    tpair = pl.BlockSpec((2, TXT, HEAD), lambda h, f: (0, 0, h))
    tall = pl.BlockSpec((2, TXT, HEAD), lambda h, f: (0, 0, h + base))
    whole = lambda *shape: pl.BlockSpec(shape, lambda h, f: (0,) * len(shape))
    in_specs = [wide] * 4 + [pair, pair, tall, whole(TXT, 1), whole(1, HEAD), whole(1, HEAD)]
    args = [q, k, v, g, lo, hi, text, keep, qg, kg]
    aliases = {}
    if before is not None:
        aliases = {len(args) + 1: 0, len(args) + 2: 1}
        in_specs += [pl.BlockSpec(memory_space=pl.ANY)] * 2
        args += list(before)
    size = (3 * TT + TXT) * TT * PER
    return pl.pallas_call(
        attend_kernel,
        grid_spec=pltpu.PrefetchScalarGridSpec(
            num_scalar_prefetch=1,
            grid=(PER,),
            in_specs=in_specs,
            out_specs=[wide, wide, pair, pair, pair, tpair, whole(8, HEAD)],
            scratch_shapes=[
                pltpu.VMEM((3 * TT + TXT, TT), F32),
                pltpu.VMEM((3 * TT + TXT, TT), BF16),
                pltpu.VMEM((3 * TT + TXT, TT), BF16),
            ],
        ),
        out_shape=[
            jax.ShapeDtypeStruct((TT, W), BF16),
            jax.ShapeDtypeStruct((TT, W), BF16),
            jax.ShapeDtypeStruct((2, TT, CW), F32),
            jax.ShapeDtypeStruct((2, TT, CW), BF16),
            jax.ShapeDtypeStruct((2, TT, CW), BF16),
            jax.ShapeDtypeStruct((2, TXT, CW), F32),
            jax.ShapeDtypeStruct((8, HEAD), F32),
        ],
        input_output_aliases=aliases,
        compiler_params=pltpu.CompilerParams(vmem_limit_bytes=40 * 2**20),
        cost_estimate=pl.CostEstimate(flops=12 * 2 * HEAD * size, bytes_accessed=14 * TT * CW * 2, transcendentals=size),
    )(flags, *args)


def finish_kernel(k_ref, own_ref, a_ref, b_ref, kg_ref, *rest):
    gk_ref, gv_ref = rest[-2:]
    k, inv, hat, _ = normed(k_ref[...], kg_ref[...])
    dk = own_ref[0] + a_ref[0].astype(F32) + b_ref[0].astype(F32)
    u = dk * kg_ref[...]
    gk_ref[...] = (inv * u - hat * (inv * inv) * jnp.mean(u * k, -1, keepdims=True)).astype(BF16)
    gv_ref[...] = (own_ref[1] + a_ref[1].astype(F32) + b_ref[1].astype(F32)).astype(BF16)


def finish(chunk, k, own, a, b, kg, before):
    base = chunk * PER
    wide = pl.BlockSpec((TT, HEAD), lambda h: (0, h + base))
    pair = pl.BlockSpec((2, TT, HEAD), lambda h: (0, 0, h))
    in_specs = [wide, pair, pair, pair, pl.BlockSpec((1, HEAD), lambda h: (0, 0))]
    args = [k, own, a, b, kg]
    aliases = {}
    if before is not None:
        aliases = {len(args): 0, len(args) + 1: 1}
        in_specs += [pl.BlockSpec(memory_space=pl.ANY)] * 2
        args += list(before)
    return pl.pallas_call(
        finish_kernel,
        grid=(PER,),
        in_specs=in_specs,
        out_specs=[wide, wide],
        out_shape=[jax.ShapeDtypeStruct((TT, W), BF16)] * 2,
        input_output_aliases=aliases,
        cost_estimate=pl.CostEstimate(flops=20 * TT * CW, bytes_accessed=22 * TT * CW, transcendentals=TT),
    )(*args)


def send(x, pairs):
    return lax.ppermute(x, "tile", pairs)


def gather_text(x):
    x = x[None]
    for dim in (3, 2, 1, 0):
        got = [x] + [send(x, steps_along(dim, by)) for by in range(1, SIZES[dim])]
        x = jnp.concatenate(got, 0)
    return x


def reduce_text(x, extra):
    width = x.shape[-1]
    slots = x.reshape(64, -1)
    tail = extra.reshape(1, -1)
    for dim in (3, 1, 2, 0):
        size = SIZES[dim]
        n = slots.shape[0]
        left = [d for d in (0, 1, 2, 3) if not (dim == 1 and d == 3) and not (dim == 2 and d in (3, 1)) and not (dim == 0 and d in (3, 1, 2))]
        shape = [SIZES[d] for d in left]
        at = left.index(dim)
        view = jnp.moveaxis(slots.reshape(shape + [-1]), at, 0).reshape(size, n // size, -1)
        total, total_tail = view[0], tail
        for by in range(1, size):
            pack = jnp.concatenate([view[by].reshape(-1), tail.reshape(-1)])
            got = send(pack, steps_along(dim, -by))
            total = total + got[: total.size].reshape(total.shape)
            total_tail = total_tail + got[total.size :].reshape(tail.shape)
        slots, tail = total, total_tail
    return slots.reshape(2, width), tail.reshape(-1)


def per_device(query, key, value, text_key, text_value, text_len, window, query_gain, key_gain, grad_out):
    me = lax.axis_index("tile")
    up = [(i, i + 1) for i in range(63)]
    down = [(i + 1, i) for i in range(63)]
    q, k, v, g = query[0], key[0], value[0], grad_out[0]
    bits = lax.dynamic_index_in_dim(window[0], me, 0, keepdims=False)
    flags = jnp.stack([((bits[0] > 0) & (me > 0)).astype(jnp.int32), ((bits[1] > 0) & (me < 63)).astype(jnp.int32)])
    qg, kg = query_gain.reshape(1, HEAD), key_gain.reshape(1, HEAD)

    los, his = [], []
    for c in range(CHUNKS):
        cols = slice(c * CW, (c + 1) * CW)
        pack = jnp.stack([k[:, cols], v[:, cols]])
        los.append(send(pack, up))
        his.append(send(pack, down))

    tkv = jnp.stack([text_key[0], text_value[0]])
    tall = gather_text(tkv.reshape(-1, HEAD)).reshape(64, 2, 2, W)
    text = tall.transpose(1, 0, 2, 3).reshape(2, TXT, W)
    slot = jnp.arange(64)
    mine = (me // 32, me // 8 % 4, me // 2 % 4, me % 2)
    back = (slot // 32, slot // 8 % 4, slot // 2 % 4, slot % 2)
    owner = place_of(*[(m - b) % s for m, b, s in zip(mine, back, SIZES)])
    index = (owner[:, None] * 2 + jnp.arange(2)[None, :]).reshape(TXT, 1)
    keep = (index < text_len[0]).astype(F32)

    outs = None
    parts, gains = [], 0.0
    for c in range(CHUNKS):
        att, gq, own, dlo, dhi, dt, gain = attend(c, flags, q, k, v, g, los[c], his[c], text, keep, qg, kg, outs)
        outs = (att, gq)
        gains = gains + gain[:2]
        from_upper = send(dlo, down)
        from_lower = send(dhi, up)
        parts.append((own, from_upper, from_lower, dt))
    fins = None
    for c in range(CHUNKS):
        own, a, b, dt = parts[c]
        fins = finish(c, k, own, a, b, kg, fins)

    dt = jnp.concatenate([p[3] for p in parts], -1)
    dt = dt.reshape(2, 64, 2, W).transpose(1, 0, 2, 3).reshape(64, 1, 4 * W)
    mine_dt, gains = reduce_text(dt.reshape(64, 2, 2 * W), gains)
    total = gains
    for by in range(1, 4):
        total = total + lax.ppermute(gains, "dp", [(i, (i + by) % 4) for i in range(4)])
    mine_dt = mine_dt.reshape(2, 2, W)
    dtn, dtv = mine_dt[0], mine_dt[1]
    heads = lambda x: x.reshape(2, HEADS, HEAD)
    t = heads(text_key[0].astype(F32))
    inv = lax.rsqrt(jnp.mean(t * t, -1, keepdims=True) + 1e-06)
    u = heads(dtn) * key_gain
    gtk = (inv * u - t * inv**3 * jnp.mean(u * t, -1, keepdims=True)).reshape(2, W)
    return (
        outs[0][None],
        outs[1][None],
        fins[0][None],
        fins[1][None],
        gtk[None],
        dtv[None],
        total[:HEAD],
        total[HEAD:],
    )


def solution(mesh):
    row = P("dp", "tile", None)
    in_specs = (row, row, row, row, row, P("dp"), P("dp", None, None), P(), P(), row)
    out_specs = (row, row, row, row, row, row, P(), P())
    return jax.shard_map(per_device, mesh=mesh, in_specs=in_specs, out_specs=out_specs, check_vma=False)
```

```python
import functools
import math

import jax
import jax.numpy as jnp
from jax import lax
from jax.experimental import pallas as pl
from jax.experimental.pallas import tpu as pltpu
from jax.sharding import PartitionSpec as P

HEADS = 12
HEAD = 128
TT = 384
TXT = 128
W = HEADS * HEAD
SPLIT = ((0, 6), (6, 12))
SCALE = HEAD ** (-0.5)
LEAD = 2
BIG = 1e30
F32 = jnp.float32
BF16 = jnp.bfloat16

SIZES = (2, 4, 4, 2)


def place_of(zh, x, y, c):
    return ((zh * 4 + x) * 4 + y) * 2 + c


def steps_along(dim, by):
    pairs = []
    for i in range(64):
        at = [i // 32, i // 8 % 4, i // 2 % 4, i % 2]
        to = list(at)
        to[dim] = (at[dim] + by) % SIZES[dim]
        pairs.append((i, place_of(*to)))
    return pairs


def nt(a, b):
    return lax.dot_general(a, b, (((1,), (1,)), ((), ())), preferred_element_type=F32)


def nn(a, b):
    return lax.dot_general(a, b, (((1,), (0,)), ((), ())), preferred_element_type=F32)


def normed(x, gain):
    x = x.astype(F32)
    inv = lax.rsqrt(jnp.mean(x * x, -1, keepdims=True) + 1e-06)
    hat = x * inv
    return x, inv, hat, (hat * gain).astype(BF16)


def attend_kernel(steps, last, flags, *refs):
    gain_ref = refs[-3]
    step = pl.program_id(0)

    def work():
        totals = [[], []]
        one, two = [attend_head(n, flags, refs, totals[n]) for n in range(2)]
        for _ in range(LEAD):
            next(one)
        alive = [one, two]
        while alive:
            for head in list(alive):
                if next(head, None) is None:
                    alive.remove(head)
        gains = totals[0][0] + totals[1][0]

        @pl.when(step == 0)
        def _():
            gain_ref[...] = gains + refs[11][...] if last else gains

        @pl.when(step > 0)
        def _():
            gain_ref[...] += gains

    if not last:
        work()
        return

    @pl.when(step < steps)
    def _():
        work()

    @pl.when(step == steps)
    def _():
        for ref in refs[-5:-3]:
            for i in range(8):
                for n in range(4):
                    ref[n, i] = jnp.broadcast_to(gain_ref[i : i + 1, :], (8, HEAD))


def attend_head(n, flags, refs, totals):
    q_ref, k_ref, v_ref, g_ref, in_ref, out_ref, t0_ref, t1_ref, keep_ref, qg_ref, kg_ref = refs[:11]
    att_ref, gq_ref, own_ref, din_ref, dout_ref, dt0_ref, dt1_ref, _, s_ref, p_ref = refs[-10:]
    cols = slice(n * HEAD, (n + 1) * HEAD)
    qg, kg = qg_ref[...], kg_ref[...]
    q, q_inv, q_hat, qn = normed(q_ref[:, cols], qg)
    scaled = qn.astype(F32) * (SCALE * math.log2(math.e))
    high = scaled.astype(BF16)
    low = (scaled - high.astype(F32)).astype(BF16)
    queries = jnp.concatenate([high, low], 1)
    inner, outer = flags[0] > 0, flags[1] > 0

    texts = [jnp.concatenate([t_ref[4 * n + 2 * i + j] for j in range(2) for t_ref in (t0_ref, t1_ref)], 0) for i in range(2)]
    raw = (in_ref[0, :, cols], k_ref[:, cols], out_ref[0, :, cols], texts[0])
    vals = (in_ref[1, :, cols], v_ref[:, cols], out_ref[1, :, cols], texts[1])
    rows = (TT, TT, TT, TXT)
    at = [pl.ds(b * TT, rows[b]) for b in range(4)]

    hats, keys, tops = [], [], []
    for b in range(4):
        _, _, hat, kn = normed(raw[b], kg)
        hats.append(hat)
        keys.append(kn)
        s = nt(jnp.concatenate([kn, kn], 1), queries)
        if b == 3:
            s = jnp.where(keep_ref[...] > 0, s, -BIG)
        s_ref[n, at[b], :] = s
        top = jnp.max(s, 0, keepdims=True)
        if b == 0:
            top = jnp.where(inner, top, -BIG)
        if b == 2:
            top = jnp.where(outer, top, -BIG)
        tops.append(top)
        yield 0
    top = jnp.maximum(jnp.maximum(tops[0], tops[1]), jnp.maximum(tops[2], tops[3]))
    total = jnp.zeros((1, TT), F32)
    for b in range(4):
        shift = top
        if b == 0:
            shift = jnp.where(inner, top, BIG)
        if b == 2:
            shift = jnp.where(outer, top, BIG)
        e = jnp.exp2(s_ref[n, at[b], :] - shift)
        s_ref[n, at[b], :] = e
        total += jnp.sum(e, 0, keepdims=True)
        yield 0
    part = 1.0 / total
    out = jnp.zeros((HEAD, TT), F32)
    for b in range(4):
        p16 = (s_ref[n, at[b], :] * part).astype(BF16)
        p_ref[n, at[b], :] = p16
        out += nn(vals[b].T, p16)
        yield 0
    att = out.T.astype(BF16)
    att_ref[:, cols] = att

    g = g_ref[:, cols]
    delta = jnp.sum(g.astype(F32) * att.astype(F32), -1, keepdims=True)
    lane = lax.broadcasted_iota(jnp.int32, (TT, HEAD), 1)
    d1 = delta.astype(BF16).astype(F32)
    d2 = (delta - d1).astype(BF16).astype(F32)
    d3 = delta - d1 - d2
    extra = jnp.where(lane == 0, -d1, jnp.where(lane == 1, -d2, jnp.where(lane == 2, -d3, 0.0)))
    cot = jnp.concatenate([g, extra.astype(BF16)], 1)
    dq = jnp.zeros((HEAD, TT), F32)
    gain_k = jnp.zeros((1, HEAD), F32)
    for b in range(4):
        ones = (lax.broadcasted_iota(jnp.int32, (rows[b], HEAD), 1) < 3).astype(F32).astype(BF16)
        dp = nt(jnp.concatenate([vals[b], ones], 1), cot)
        ds = (s_ref[n, at[b], :] * part * dp).astype(BF16)
        dv = nn(p_ref[n, at[b], :], g)
        dk = nn(ds, qn) * SCALE
        dq += nn(keys[b].T, ds)
        gain_k += jnp.sum(dk * hats[b], 0, keepdims=True)
        if b < 3:
            into = (din_ref, own_ref, dout_ref)[b]
            into[0, :, cols] = dk.astype(into.dtype)
            into[1, :, cols] = dv.astype(into.dtype)
        else:
            for i, x in enumerate((dk, dv)):
                for j in range(2):
                    for m in range(4):
                        first = j * 64 + m * 8
                        dt0_ref[m, 4 * n + 2 * i + j] = x[first : first + 8]
                        dt1_ref[m, 4 * n + 2 * i + j] = x[first + 32 : first + 40]
        yield 0
    dqn = dq.T * SCALE
    u = dqn * qg
    gq_ref[:, cols] = (q_inv * u - q_hat * (q_inv * q_inv) * jnp.mean(u * q, -1, keepdims=True)).astype(BF16)
    gain_q = jnp.sum(dqn * q_hat, 0, keepdims=True)
    row = lax.broadcasted_iota(jnp.int32, (8, HEAD), 0)
    totals.append(jnp.where(row == 0, gain_q, jnp.where(row == 1, gain_k, 0.0)))
    yield 0


def attend(chunk, flags, q, k, v, g, inner, outer, texts, keep, qg, kg, before):
    base, end = SPLIT[chunk]
    heads, last = end - base, before is not None
    steps, base = heads // 2, base // 2
    at = lambda h: jnp.minimum(h, steps - 1)
    wide = pl.BlockSpec((TT, 2 * HEAD), lambda h, f: (0, at(h) + base))
    pair = pl.BlockSpec((2, TT, 2 * HEAD), lambda h, f: (0, 0, at(h)))
    tall = pl.BlockSpec((8, 32, HEAD), lambda h, f: (at(h) + base, 0, 0))
    half = pl.BlockSpec((4, 8, 8, HEAD), lambda h, f: (0, h + base, 0, 0))
    whole = lambda *shape: pl.BlockSpec(shape, lambda h, f: (0,) * len(shape))
    in_specs = [wide] * 4 + [pair, pair, tall, tall, whole(TXT, 1), whole(1, HEAD), whole(1, HEAD)]
    args = [q, k, v, g, inner, outer, *texts, keep, qg, kg]
    aliases = {}
    if last:
        in_specs += [whole(8, HEAD)] + [pl.BlockSpec(memory_space=pl.ANY)] * 4
        aliases = {len(args) + 2: 0, len(args) + 3: 1, len(args) + 4: 5, len(args) + 5: 6}
        args += [before[7], before[0], before[1], before[5], before[6]]
    size = (3 * TT + TXT) * TT * heads
    width = heads * HEAD
    return pl.pallas_call(
        functools.partial(attend_kernel, steps, last),
        grid_spec=pltpu.PrefetchScalarGridSpec(
            num_scalar_prefetch=1,
            grid=(steps + last,),
            in_specs=in_specs,
            out_specs=[wide, wide, pair, pair, pair, half, half, whole(8, HEAD)],
            scratch_shapes=[
                pltpu.VMEM((2, 3 * TT + TXT, TT), F32),
                pltpu.VMEM((2, 3 * TT + TXT, TT), BF16),
            ],
        ),
        out_shape=[
            jax.ShapeDtypeStruct((TT, W), BF16),
            jax.ShapeDtypeStruct((TT, W), BF16),
            jax.ShapeDtypeStruct((2, TT, width), F32),
            jax.ShapeDtypeStruct((2, TT, width), BF16),
            jax.ShapeDtypeStruct((2, TT, width), BF16),
            jax.ShapeDtypeStruct((4, 4 * HEADS + 8, 8, HEAD), F32),
            jax.ShapeDtypeStruct((4, 4 * HEADS + 8, 8, HEAD), F32),
            jax.ShapeDtypeStruct((8, HEAD), F32),
        ],
        input_output_aliases=aliases,
        compiler_params=pltpu.CompilerParams(vmem_limit_bytes=60 * 2**20),
        cost_estimate=pl.CostEstimate(flops=24 * HEAD * size, bytes_accessed=18 * TT * width, transcendentals=size),
    )(flags, *args)


def finish_kernel(k_ref, own_ref, a_ref, b_ref, kg_ref, *rest):
    gk_ref, gv_ref = rest[-2:]
    for n in range(2):
        cols = slice(n * HEAD, (n + 1) * HEAD)
        k, inv, hat, _ = normed(k_ref[:, cols], kg_ref[...])
        dk, dv = [own_ref[i, :, cols] + a_ref[i, :, cols].astype(F32) + b_ref[i, :, cols].astype(F32) for i in range(2)]
        u = dk * kg_ref[...]
        gk_ref[:, cols] = (inv * u - hat * (inv * inv) * jnp.mean(u * k, -1, keepdims=True)).astype(BF16)
        gv_ref[:, cols] = dv.astype(BF16)


def finish(chunk, k, own, a, b, kg, before):
    base, end = SPLIT[chunk]
    heads = end - base
    wide = pl.BlockSpec((TT, 2 * HEAD), lambda h: (0, h + base // 2))
    pair = pl.BlockSpec((2, TT, 2 * HEAD), lambda h: (0, 0, h))
    in_specs = [wide, pair, pair, pair, pl.BlockSpec((1, HEAD), lambda h: (0, 0))]
    args = [k, own, a, b, kg]
    aliases = {}
    if before is not None:
        aliases = {len(args): 0, len(args) + 1: 1}
        in_specs += [pl.BlockSpec(memory_space=pl.ANY)] * 2
        args += list(before)
    return pl.pallas_call(
        finish_kernel,
        grid=(heads // 2,),
        in_specs=in_specs,
        out_specs=[wide, wide],
        out_shape=[jax.ShapeDtypeStruct((TT, W), BF16)] * 2,
        input_output_aliases=aliases,
        compiler_params=pltpu.CompilerParams(vmem_limit_bytes=60 * 2**20),
        cost_estimate=pl.CostEstimate(flops=20 * TT * heads * HEAD, bytes_accessed=26 * TT * heads * HEAD, transcendentals=TT),
    )(*args)


def send(x, pairs):
    return lax.ppermute(x, "tile", pairs)


INNER = [(i, i ^ 1) for i in range(64)]
OUTER = [(i, (i - 1 ^ 1) + 1) for i in range(1, 63)]


def after(x, *others):
    for other in others:
        zero = jnp.minimum(jnp.abs(other[(-1,) * other.ndim]), 0).astype(x.dtype)
        x = x + zero
    return x


def gather_all(x, packs):
    x = x[None]
    got = send(x, steps_along(0, 1))
    pack = after(packs[0], got)
    inners, outers = [send(pack, INNER)], [send(pack, OUTER)]
    x = jnp.concatenate([x, got], 0)
    stage = [send(x, steps_along(1, by)) for by in range(1, 4)]
    x = jnp.stack([x] + stage)
    stage = [send(x, steps_along(2, by)) for by in range(1, 4)]
    x = jnp.stack([x] + stage)
    pack = after(packs[1], *stage)
    inners.append(send(pack, INNER))
    outers.append(send(pack, OUTER))
    x = x.transpose(3, 1, 0, 2, 4).reshape(4 * HEADS, 32, HEAD)
    return (x, send(x, steps_along(3, 1))), inners, outers


def reduce_text(mine, other, first, second):
    total = mine + send(other, steps_along(3, -1))
    total = after(total, *first)
    for dim in (1, 2, 0):
        if dim == 1:
            parts = [total[i] for i in range(4)]
        else:
            if dim == 0:
                total = after(total, *second)
            n = total.shape[1] // SIZES[dim]
            parts = [total[:, i * n : (i + 1) * n] for i in range(SIZES[dim])]
        got = [send(parts[by], steps_along(dim, -by)) for by in range(1, SIZES[dim])]
        total = functools.reduce(jnp.add, got, parts[0])
    return total[:, 0]


def per_device(query, key, value, text_key, text_value, text_len, window, query_gain, key_gain, grad_out):
    me = lax.axis_index("tile")
    q, k, v, g = query[0], key[0], value[0], grad_out[0]
    bits = lax.dynamic_index_in_dim(window[0], me, 0, keepdims=False)
    below, above = (bits[0] > 0) & (me > 0), (bits[1] > 0) & (me < 63)
    even = me % 2 == 0
    flags = jnp.stack([jnp.where(even, above, below), jnp.where(even, below, above)]).astype(jnp.int32)
    qg, kg = query_gain.reshape(1, HEAD), key_gain.reshape(1, HEAD)

    rows = jnp.stack([text_key[0], text_value[0]]).reshape(2, 2, HEADS, HEAD).transpose(2, 0, 1, 3).reshape(4 * HEADS, HEAD)
    packs = [jnp.stack([k[:, a * HEAD : b * HEAD], v[:, a * HEAD : b * HEAD]]) for a, b in SPLIT]
    texts, inners, outers = gather_all(rows, packs)
    slot = jnp.arange(64)
    here = (me // 32, me // 8 % 4, me // 2 % 4, me % 2)
    back = (slot % 2, slot // 8 % 4, slot // 2 % 4, slot // 32)
    owner = place_of(*[(m - b) % s for m, b, s in zip(here, back, SIZES)])
    index = (owner[None, :] * 2 + jnp.arange(2)[:, None]).reshape(TXT, 1)
    keep = (index < text_len[0]).astype(F32)

    outs, parts = None, []
    for c in range(len(SPLIT)):
        outs = attend(c, flags, q, k, v, g, inners[c], outers[c], texts, keep, qg, kg, outs)
        own, din, dout = outs[2:5]
        parts.append((own, send(din, INNER), send(dout, OUTER)))
    summed = reduce_text(outs[5], outs[6], parts[0][1:], parts[1][1:])
    fins = None
    for c in range(len(SPLIT)):
        fins = finish(c, k, *parts[c], kg, fins)

    gains = summed[4 * HEADS : 4 * HEADS + 2]
    total = gains
    for by in range(1, 4):
        total = total + lax.ppermute(gains, "dp", [(i, (i + by) % 4) for i in range(4)])
    dtn, dtv = [summed[: 4 * HEADS].reshape(HEADS, 2, 2, HEAD)[:, i].transpose(1, 0, 2) for i in range(2)]
    t = text_key[0].astype(F32).reshape(2, HEADS, HEAD)
    inv = lax.rsqrt(jnp.mean(t * t, -1, keepdims=True) + 1e-06)
    u = dtn * key_gain
    gtk = (inv * u - t * inv**3 * jnp.mean(u * t, -1, keepdims=True)).reshape(1, 2, W)
    return (
        outs[0][None],
        outs[1][None],
        fins[0][None],
        fins[1][None],
        gtk,
        dtv.reshape(1, 2, W),
        total[0],
        total[1],
    )


def solution(mesh):
    row = P("dp", "tile", None)
    in_specs = (row, row, row, row, row, P("dp"), P("dp", None, None), P(), P(), row)
    out_specs = (row, row, row, row, row, row, P(), P())
    return jax.shard_map(per_device, mesh=mesh, in_specs=in_specs, out_specs=out_specs, check_vma=False)
```

```python
import functools
import math

import jax
import jax.numpy as jnp
from jax import lax
from jax.experimental import pallas as pl
from jax.experimental.pallas import tpu as pltpu
from jax.sharding import PartitionSpec as P

HEADS = 12
HEAD = 128
TT = 384
TXT = 128
W = HEADS * HEAD
SPLIT = ((0, 6), (6, 12))
SCALE = HEAD ** (-0.5)
LEAD = 2
BIG = 1e30
F32 = jnp.float32
BF16 = jnp.bfloat16

SIZES = (2, 4, 4, 2)


def place_of(zh, x, y, c):
    return ((zh * 4 + x) * 4 + y) * 2 + c


def steps_along(dim, by):
    pairs = []
    for i in range(64):
        at = [i // 32, i // 8 % 4, i // 2 % 4, i % 2]
        to = list(at)
        to[dim] = (at[dim] + by) % SIZES[dim]
        pairs.append((i, place_of(*to)))
    return pairs


def nt(a, b):
    return lax.dot_general(a, b, (((1,), (1,)), ((), ())), preferred_element_type=F32)


def nn(a, b):
    return lax.dot_general(a, b, (((1,), (0,)), ((), ())), preferred_element_type=F32)


def normed(x, gain):
    x = x.astype(F32)
    inv = lax.rsqrt(jnp.mean(x * x, -1, keepdims=True) + 1e-06)
    hat = x * inv
    return x, inv, hat, (hat * gain).astype(BF16)


def attend_kernel(steps, last, flags, *refs):
    gain_ref = refs[-3]
    step = pl.program_id(0)

    def work():
        totals = [[], []]
        one, two = [attend_head(n, flags, refs, totals[n]) for n in range(2)]
        for _ in range(LEAD):
            next(one)
        alive = [one, two]
        while alive:
            for head in list(alive):
                if next(head, None) is None:
                    alive.remove(head)
        gains = totals[0][0] + totals[1][0]

        @pl.when(step == 0)
        def _():
            gain_ref[...] = gains + refs[11][...] if last else gains

        @pl.when(step > 0)
        def _():
            gain_ref[...] += gains

    if not last:
        work()
        return

    @pl.when(step < steps)
    def _():
        work()

    @pl.when(step == steps)
    def _():
        for ref in refs[-5:-3]:
            for i in range(8):
                for n in range(4):
                    ref[n, i] = jnp.broadcast_to(gain_ref[i : i + 1, :], (8, HEAD))


def attend_head(n, flags, refs, totals):
    q_ref, k_ref, v_ref, g_ref, in_ref, out_ref, t0_ref, t1_ref, keep_ref, qg_ref, kg_ref = refs[:11]
    att_ref, gq_ref, own_ref, din_ref, dout_ref, dt0_ref, dt1_ref, _, s_ref, p_ref = refs[-10:]
    cols = slice(n * HEAD, (n + 1) * HEAD)
    qg, kg = qg_ref[...], kg_ref[...]
    q, q_inv, q_hat, qn = normed(q_ref[:, cols], qg)
    scaled = qn.astype(F32) * (SCALE * math.log2(math.e))
    high = scaled.astype(BF16)
    low = (scaled - high.astype(F32)).astype(BF16)
    queries = jnp.concatenate([high, low], 1)
    inner, outer = flags[0] > 0, flags[1] > 0

    texts = [jnp.concatenate([t_ref[4 * n + 2 * i + j] for j in range(2) for t_ref in (t0_ref, t1_ref)], 0) for i in range(2)]
    raw = (in_ref[0, :, cols], k_ref[:, cols], out_ref[0, :, cols], texts[0])
    vals = (in_ref[1, :, cols], v_ref[:, cols], out_ref[1, :, cols], texts[1])
    rows = (TT, TT, TT, TXT)
    at = [pl.ds(b * TT, rows[b]) for b in range(4)]

    hats, keys, tops = [], [], []
    for b in range(4):
        _, _, hat, kn = normed(raw[b], kg)
        hats.append(hat)
        keys.append(kn)
        s = nt(jnp.concatenate([kn, kn], 1), queries)
        if b == 3:
            s = jnp.where(keep_ref[...] > 0, s, -BIG)
        s_ref[n, at[b], :] = s
        top = jnp.max(s, 0, keepdims=True)
        if b == 0:
            top = jnp.where(inner, top, -BIG)
        if b == 2:
            top = jnp.where(outer, top, -BIG)
        tops.append(top)
        yield 0
    top = jnp.maximum(jnp.maximum(tops[0], tops[1]), jnp.maximum(tops[2], tops[3]))
    total = jnp.zeros((1, TT), F32)
    for b in range(4):
        shift = top
        if b == 0:
            shift = jnp.where(inner, top, BIG)
        if b == 2:
            shift = jnp.where(outer, top, BIG)
        e = jnp.exp2(s_ref[n, at[b], :] - shift)
        s_ref[n, at[b], :] = e
        total += jnp.sum(e, 0, keepdims=True)
        yield 0
    part = 1.0 / total
    out = jnp.zeros((HEAD, TT), F32)
    for b in range(4):
        p16 = (s_ref[n, at[b], :] * part).astype(BF16)
        p_ref[n, at[b], :] = p16
        out += nn(vals[b].T, p16)
        yield 0
    att = out.T.astype(BF16)
    att_ref[:, cols] = att

    g = g_ref[:, cols]
    delta = jnp.sum(g.astype(F32) * att.astype(F32), -1, keepdims=True)
    lane = lax.broadcasted_iota(jnp.int32, (TT, HEAD), 1)
    d1 = delta.astype(BF16).astype(F32)
    d2 = (delta - d1).astype(BF16).astype(F32)
    d3 = delta - d1 - d2
    extra = jnp.where(lane == 0, -d1, jnp.where(lane == 1, -d2, jnp.where(lane == 2, -d3, 0.0)))
    cot = jnp.concatenate([g, extra.astype(BF16)], 1)
    dq = jnp.zeros((HEAD, TT), F32)
    gain_k = jnp.zeros((1, HEAD), F32)
    for b in range(4):
        ones = (lax.broadcasted_iota(jnp.int32, (rows[b], HEAD), 1) < 3).astype(F32).astype(BF16)
        dp = nt(jnp.concatenate([vals[b], ones], 1), cot)
        ds = (s_ref[n, at[b], :] * part * dp).astype(BF16)
        dv = nn(p_ref[n, at[b], :], g)
        dk = nn(ds, qn) * SCALE
        dq += nn(keys[b].T, ds)
        gain_k += jnp.sum(dk * hats[b], 0, keepdims=True)
        if b < 3:
            into = (din_ref, own_ref, dout_ref)[b]
            into[0, :, cols] = dk.astype(into.dtype)
            into[1, :, cols] = dv.astype(into.dtype)
        else:
            for i, x in enumerate((dk, dv)):
                for j in range(2):
                    for m in range(4):
                        first = j * 64 + m * 8
                        dt0_ref[m, 4 * n + 2 * i + j] = x[first : first + 8]
                        dt1_ref[m, 4 * n + 2 * i + j] = x[first + 32 : first + 40]
        yield 0
    dqn = dq.T * SCALE
    u = dqn * qg
    gq_ref[:, cols] = (q_inv * u - q_hat * (q_inv * q_inv) * jnp.mean(u * q, -1, keepdims=True)).astype(BF16)
    gain_q = jnp.sum(dqn * q_hat, 0, keepdims=True)
    row = lax.broadcasted_iota(jnp.int32, (8, HEAD), 0)
    totals.append(jnp.where(row == 0, gain_q, jnp.where(row == 1, gain_k, 0.0)))
    yield 0


def attend(chunk, flags, q, k, v, g, inner, outer, texts, keep, qg, kg, before):
    base, end = SPLIT[chunk]
    heads, last = end - base, before is not None
    steps, base = heads // 2, base // 2
    at = lambda h: jnp.minimum(h, steps - 1)
    wide = pl.BlockSpec((TT, 2 * HEAD), lambda h, f: (0, at(h) + base))
    pair = pl.BlockSpec((2, TT, 2 * HEAD), lambda h, f: (0, 0, at(h)))
    tall = pl.BlockSpec((8, 32, HEAD), lambda h, f: (at(h) + base, 0, 0))
    half = pl.BlockSpec((4, 8, 8, HEAD), lambda h, f: (0, h + base, 0, 0))
    whole = lambda *shape: pl.BlockSpec(shape, lambda h, f: (0,) * len(shape))
    in_specs = [wide] * 4 + [pair, pair, tall, tall, whole(TXT, 1), whole(1, HEAD), whole(1, HEAD)]
    args = [q, k, v, g, inner, outer, *texts, keep, qg, kg]
    aliases = {}
    if last:
        in_specs += [whole(8, HEAD)] + [pl.BlockSpec(memory_space=pl.ANY)] * 4
        aliases = {len(args) + 2: 0, len(args) + 3: 1, len(args) + 4: 5, len(args) + 5: 6}
        args += [before[7], before[0], before[1], before[5], before[6]]
    size = (3 * TT + TXT) * TT * heads
    width = heads * HEAD
    return pl.pallas_call(
        functools.partial(attend_kernel, steps, last),
        grid_spec=pltpu.PrefetchScalarGridSpec(
            num_scalar_prefetch=1,
            grid=(steps + last,),
            in_specs=in_specs,
            out_specs=[wide, wide, pair, pair, pair, half, half, whole(8, HEAD)],
            scratch_shapes=[
                pltpu.VMEM((2, 3 * TT + TXT, TT), F32),
                pltpu.VMEM((2, 3 * TT + TXT, TT), BF16),
            ],
        ),
        out_shape=[
            jax.ShapeDtypeStruct((TT, W), BF16),
            jax.ShapeDtypeStruct((TT, W), BF16),
            jax.ShapeDtypeStruct((2, TT, width), F32),
            jax.ShapeDtypeStruct((2, TT, width), BF16),
            jax.ShapeDtypeStruct((2, TT, width), BF16),
            jax.ShapeDtypeStruct((4, 4 * HEADS + 8, 8, HEAD), F32),
            jax.ShapeDtypeStruct((4, 4 * HEADS + 8, 8, HEAD), F32),
            jax.ShapeDtypeStruct((8, HEAD), F32),
        ],
        input_output_aliases=aliases,
        compiler_params=pltpu.CompilerParams(vmem_limit_bytes=60 * 2**20),
        cost_estimate=pl.CostEstimate(flops=24 * HEAD * size, bytes_accessed=18 * TT * width, transcendentals=size),
    )(flags, *args)


def finish_kernel(k_ref, own_ref, a_ref, b_ref, kg_ref, *rest):
    gk_ref, gv_ref = rest[-2:]
    for n in range(2):
        cols = slice(n * HEAD, (n + 1) * HEAD)
        k, inv, hat, _ = normed(k_ref[:, cols], kg_ref[...])
        dk, dv = [own_ref[i, :, cols] + a_ref[i, :, cols].astype(F32) + b_ref[i, :, cols].astype(F32) for i in range(2)]
        u = dk * kg_ref[...]
        gk_ref[:, cols] = (inv * u - hat * (inv * inv) * jnp.mean(u * k, -1, keepdims=True)).astype(BF16)
        gv_ref[:, cols] = dv.astype(BF16)


def finish(chunk, k, own, a, b, kg, before):
    base, end = SPLIT[chunk]
    heads = end - base
    wide = pl.BlockSpec((TT, 2 * HEAD), lambda h: (0, h + base // 2))
    pair = pl.BlockSpec((2, TT, 2 * HEAD), lambda h: (0, 0, h))
    in_specs = [wide, pair, pair, pair, pl.BlockSpec((1, HEAD), lambda h: (0, 0))]
    args = [k, own, a, b, kg]
    aliases = {}
    if before is not None:
        aliases = {len(args): 0, len(args) + 1: 1}
        in_specs += [pl.BlockSpec(memory_space=pl.ANY)] * 2
        args += list(before)
    return pl.pallas_call(
        finish_kernel,
        grid=(heads // 2,),
        in_specs=in_specs,
        out_specs=[wide, wide],
        out_shape=[jax.ShapeDtypeStruct((TT, W), BF16)] * 2,
        input_output_aliases=aliases,
        compiler_params=pltpu.CompilerParams(vmem_limit_bytes=60 * 2**20),
        cost_estimate=pl.CostEstimate(flops=20 * TT * heads * HEAD, bytes_accessed=26 * TT * heads * HEAD, transcendentals=TT),
    )(*args)


def send(x, pairs):
    return lax.ppermute(x, "tile", pairs)


INNER = [(i, i ^ 1) for i in range(64)]
OUTER = [(i, (i - 1 ^ 1) + 1) for i in range(1, 63)]


def after(x, *others):
    for other in others:
        zero = jnp.minimum(jnp.abs(other[(-1,) * other.ndim]), 0).astype(x.dtype)
        x = x + zero
    return x


def gather_all(x, packs):
    x = x[None]
    got = send(x, steps_along(0, 1))
    pack = after(packs[0], got)
    inners, outers = [send(pack, INNER)], [send(pack, OUTER)]
    x = jnp.concatenate([x, got], 0)
    stage = [send(x, steps_along(1, by)) for by in range(1, 4)]
    x = jnp.stack([x] + stage)
    stage = [send(x, steps_along(2, by)) for by in range(1, 4)]
    x = jnp.stack([x] + stage)
    pack = after(packs[1], *stage)
    inners.append(send(pack, INNER))
    outers.append(send(pack, OUTER))
    x = x.transpose(3, 1, 0, 2, 4).reshape(4 * HEADS, 32, HEAD)
    return (x, send(x, steps_along(3, 1))), inners, outers


def reduce_text(mine, other, first, second):
    total = mine + send(other, steps_along(3, -1))
    for dim in (1, 2, 0):
        if dim == 1:
            parts = [total[i] for i in range(4)]
        else:
            total = after(total, *(first if dim == 2 else second))
            n = total.shape[1] // SIZES[dim]
            parts = [total[:, i * n : (i + 1) * n] for i in range(SIZES[dim])]
        got = [send(parts[by], steps_along(dim, -by)) for by in range(1, SIZES[dim])]
        total = functools.reduce(jnp.add, got, parts[0])
    return total[:, 0]


def per_device(query, key, value, text_key, text_value, text_len, window, query_gain, key_gain, grad_out):
    me = lax.axis_index("tile")
    q, k, v, g = query[0], key[0], value[0], grad_out[0]
    bits = lax.dynamic_index_in_dim(window[0], me, 0, keepdims=False)
    below, above = (bits[0] > 0) & (me > 0), (bits[1] > 0) & (me < 63)
    even = me % 2 == 0
    flags = jnp.stack([jnp.where(even, above, below), jnp.where(even, below, above)]).astype(jnp.int32)
    qg, kg = query_gain.reshape(1, HEAD), key_gain.reshape(1, HEAD)

    rows = jnp.stack([text_key[0], text_value[0]]).reshape(2, 2, HEADS, HEAD).transpose(2, 0, 1, 3).reshape(4 * HEADS, HEAD)
    packs = [jnp.stack([k[:, a * HEAD : b * HEAD], v[:, a * HEAD : b * HEAD]]) for a, b in SPLIT]
    texts, inners, outers = gather_all(rows, packs)
    slot = jnp.arange(64)
    here = (me // 32, me // 8 % 4, me // 2 % 4, me % 2)
    back = (slot % 2, slot // 8 % 4, slot // 2 % 4, slot // 32)
    owner = place_of(*[(m - b) % s for m, b, s in zip(here, back, SIZES)])
    index = (owner[None, :] * 2 + jnp.arange(2)[:, None]).reshape(TXT, 1)
    keep = (index < text_len[0]).astype(F32)

    outs, parts = None, []
    for c in range(len(SPLIT)):
        outs = attend(c, flags, q, k, v, g, inners[c], outers[c], texts, keep, qg, kg, outs)
        own, din, dout = outs[2:5]
        parts.append((own, send(din, INNER), send(dout, OUTER)))
    fins = finish(0, k, *parts[0], kg, None)
    summed = reduce_text(outs[5], outs[6], [fins[1][:1, :1]], parts[1][1:])
    fins = finish(1, k, *parts[1], kg, fins)

    gains = summed[4 * HEADS : 4 * HEADS + 2]
    total = gains
    for by in range(1, 4):
        total = total + lax.ppermute(gains, "dp", [(i, (i + by) % 4) for i in range(4)])
    dtn, dtv = [summed[: 4 * HEADS].reshape(HEADS, 2, 2, HEAD)[:, i].transpose(1, 0, 2) for i in range(2)]
    t = text_key[0].astype(F32).reshape(2, HEADS, HEAD)
    inv = lax.rsqrt(jnp.mean(t * t, -1, keepdims=True) + 1e-06)
    u = dtn * key_gain
    gtk = (inv * u - t * inv**3 * jnp.mean(u * t, -1, keepdims=True)).reshape(1, 2, W)
    return (
        outs[0][None],
        outs[1][None],
        fins[0][None],
        fins[1][None],
        gtk,
        dtv.reshape(1, 2, W),
        total[0],
        total[1],
    )


def solution(mesh):
    row = P("dp", "tile", None)
    in_specs = (row, row, row, row, row, P("dp"), P("dp", None, None), P(), P(), row)
    out_specs = (row, row, row, row, row, row, P(), P())
    return jax.shard_map(per_device, mesh=mesh, in_specs=in_specs, out_specs=out_specs, check_vma=False)
```

```python
import functools
import math

import jax
import jax.numpy as jnp
from jax import lax
from jax.experimental import pallas as pl
from jax.experimental.pallas import tpu as pltpu
from jax.sharding import PartitionSpec as P

HEADS = 12
HEAD = 128
TT = 384
TXT = 128
W = HEADS * HEAD
SPLIT = ((0, 6), (6, 12))
SCALE = HEAD ** (-0.5)
LEAD = 2
BIG = 1e30
F32 = jnp.float32
BF16 = jnp.bfloat16

SIZES = (2, 4, 4, 2)


def place_of(zh, x, y, c):
    return ((zh * 4 + x) * 4 + y) * 2 + c


def steps_along(dim, by):
    pairs = []
    for i in range(64):
        at = [i // 32, i // 8 % 4, i // 2 % 4, i % 2]
        to = list(at)
        to[dim] = (at[dim] + by) % SIZES[dim]
        pairs.append((i, place_of(*to)))
    return pairs


def nt(a, b):
    return lax.dot_general(a, b, (((1,), (1,)), ((), ())), preferred_element_type=F32)


def nn(a, b):
    return lax.dot_general(a, b, (((1,), (0,)), ((), ())), preferred_element_type=F32)


def normed(x, gain):
    x = x.astype(F32)
    inv = lax.rsqrt(jnp.mean(x * x, -1, keepdims=True) + 1e-06)
    hat = x * inv
    return x, inv, hat, (hat * gain).astype(BF16)


def attend_kernel(steps, last, flags, *refs):
    gain_ref = refs[-3]
    step = pl.program_id(0)

    def work():
        totals = [[], []]
        one, two = [attend_head(n, flags, refs, totals[n]) for n in range(2)]
        for _ in range(LEAD):
            next(one)
        alive = [one, two]
        while alive:
            for head in list(alive):
                if next(head, None) is None:
                    alive.remove(head)
        gains = totals[0][0] + totals[1][0]

        @pl.when(step == 0)
        def _():
            gain_ref[...] = gains + refs[11][...] if last else gains

        @pl.when(step > 0)
        def _():
            gain_ref[...] += gains

    if not last:
        work()
        return

    @pl.when(step < steps)
    def _():
        work()

    @pl.when(step == steps)
    def _():
        for ref in refs[-5:-3]:
            for i in range(8):
                for n in range(4):
                    ref[n, i] = jnp.broadcast_to(gain_ref[i : i + 1, :], (8, HEAD))


def attend_head(n, flags, refs, totals):
    q_ref, k_ref, v_ref, g_ref, in_ref, out_ref, t0_ref, t1_ref, keep_ref, qg_ref, kg_ref = refs[:11]
    att_ref, gq_ref, own_ref, din_ref, dout_ref, dt0_ref, dt1_ref, _, s_ref, p_ref = refs[-10:]
    cols = slice(n * HEAD, (n + 1) * HEAD)
    qg, kg = qg_ref[...], kg_ref[...]
    q, q_inv, q_hat, qn = normed(q_ref[:, cols], qg)
    scaled = qn.astype(F32) * (SCALE * math.log2(math.e))
    high = scaled.astype(BF16)
    low = (scaled - high.astype(F32)).astype(BF16)
    queries = jnp.concatenate([high, low], 1)
    inner, outer = flags[0] > 0, flags[1] > 0

    texts = [jnp.concatenate([t_ref[4 * n + 2 * i + j] for j in range(2) for t_ref in (t0_ref, t1_ref)], 0) for i in range(2)]
    raw = (in_ref[0, :, cols], k_ref[:, cols], out_ref[0, :, cols], texts[0])
    vals = (in_ref[1, :, cols], v_ref[:, cols], out_ref[1, :, cols], texts[1])
    rows = (TT, TT, TT, TXT)
    at = [pl.ds(b * TT, rows[b]) for b in range(4)]

    hats, keys, tops = [], [], []
    for b in range(4):
        _, _, hat, kn = normed(raw[b], kg)
        hats.append(hat)
        keys.append(kn)
        s = nt(jnp.concatenate([kn, kn], 1), queries)
        if b == 3:
            s = jnp.where(keep_ref[...] > 0, s, -BIG)
        s_ref[n, at[b], :] = s
        top = jnp.max(s, 0, keepdims=True)
        if b == 0:
            top = jnp.where(inner, top, -BIG)
        if b == 2:
            top = jnp.where(outer, top, -BIG)
        tops.append(top)
        yield 0
    top = jnp.maximum(jnp.maximum(tops[0], tops[1]), jnp.maximum(tops[2], tops[3]))
    total = jnp.zeros((1, TT), F32)
    for b in range(4):
        shift = top
        if b == 0:
            shift = jnp.where(inner, top, BIG)
        if b == 2:
            shift = jnp.where(outer, top, BIG)
        e = jnp.exp2(s_ref[n, at[b], :] - shift)
        s_ref[n, at[b], :] = e
        total += jnp.sum(e, 0, keepdims=True)
        yield 0
    part = 1.0 / total
    out = jnp.zeros((HEAD, TT), F32)
    for b in range(4):
        p16 = (s_ref[n, at[b], :] * part).astype(BF16)
        p_ref[n, at[b], :] = p16
        out += nn(vals[b].T, p16)
        yield 0
    att = out.T.astype(BF16)
    att_ref[:, cols] = att

    g = g_ref[:, cols]
    delta = jnp.sum(g.astype(F32) * att.astype(F32), -1, keepdims=True)
    lane = lax.broadcasted_iota(jnp.int32, (TT, HEAD), 1)
    d1 = delta.astype(BF16).astype(F32)
    d2 = (delta - d1).astype(BF16).astype(F32)
    d3 = delta - d1 - d2
    extra = jnp.where(lane == 0, -d1, jnp.where(lane == 1, -d2, jnp.where(lane == 2, -d3, 0.0)))
    cot = jnp.concatenate([g, extra.astype(BF16)], 1)
    dq = jnp.zeros((HEAD, TT), F32)
    gain_k = jnp.zeros((1, HEAD), F32)
    for b in range(4):
        ones = (lax.broadcasted_iota(jnp.int32, (rows[b], HEAD), 1) < 3).astype(F32).astype(BF16)
        dp = nt(jnp.concatenate([vals[b], ones], 1), cot)
        ds = (s_ref[n, at[b], :] * part * dp).astype(BF16)
        dv = nn(p_ref[n, at[b], :], g)
        dk = nn(ds, qn) * SCALE
        dq += nn(keys[b].T, ds)
        gain_k += jnp.sum(dk * hats[b], 0, keepdims=True)
        if b < 3:
            into = (din_ref, own_ref, dout_ref)[b]
            into[0, :, cols] = dk.astype(into.dtype)
            into[1, :, cols] = dv.astype(into.dtype)
        else:
            for i, x in enumerate((dk, dv)):
                for j in range(2):
                    for m in range(4):
                        first = j * 64 + m * 8
                        dt0_ref[m, 4 * n + 2 * i + j] = x[first : first + 8]
                        dt1_ref[m, 4 * n + 2 * i + j] = x[first + 32 : first + 40]
        yield 0
    dqn = dq.T * SCALE
    u = dqn * qg
    gq_ref[:, cols] = (q_inv * u - q_hat * (q_inv * q_inv) * jnp.mean(u * q, -1, keepdims=True)).astype(BF16)
    gain_q = jnp.sum(dqn * q_hat, 0, keepdims=True)
    row = lax.broadcasted_iota(jnp.int32, (8, HEAD), 0)
    totals.append(jnp.where(row == 0, gain_q, jnp.where(row == 1, gain_k, 0.0)))
    yield 0


def attend(chunk, flags, q, k, v, g, inner, outer, texts, keep, qg, kg, before):
    base, end = SPLIT[chunk]
    heads, last = end - base, before is not None
    steps, base = heads // 2, base // 2
    at = lambda h: jnp.minimum(h, steps - 1)
    wide = pl.BlockSpec((TT, 2 * HEAD), lambda h, f: (0, at(h) + base))
    pair = pl.BlockSpec((2, TT, 2 * HEAD), lambda h, f: (0, 0, at(h)))
    tall = pl.BlockSpec((8, 32, HEAD), lambda h, f: (at(h) + base, 0, 0))
    half = pl.BlockSpec((4, 8, 8, HEAD), lambda h, f: (0, h + base, 0, 0))
    whole = lambda *shape: pl.BlockSpec(shape, lambda h, f: (0,) * len(shape))
    in_specs = [wide] * 4 + [pair, pair, tall, tall, whole(TXT, 1), whole(1, HEAD), whole(1, HEAD)]
    args = [q, k, v, g, inner, outer, *texts, keep, qg, kg]
    aliases = {}
    if last:
        in_specs += [whole(8, HEAD)] + [pl.BlockSpec(memory_space=pl.ANY)] * 4
        aliases = {len(args) + 2: 0, len(args) + 3: 1, len(args) + 4: 5, len(args) + 5: 6}
        args += [before[7], before[0], before[1], before[5], before[6]]
    size = (3 * TT + TXT) * TT * heads
    width = heads * HEAD
    return pl.pallas_call(
        functools.partial(attend_kernel, steps, last),
        grid_spec=pltpu.PrefetchScalarGridSpec(
            num_scalar_prefetch=1,
            grid=(steps + last,),
            in_specs=in_specs,
            out_specs=[wide, wide, pair, pair, pair, half, half, whole(8, HEAD)],
            scratch_shapes=[
                pltpu.VMEM((2, 3 * TT + TXT, TT), F32),
                pltpu.VMEM((2, 3 * TT + TXT, TT), BF16),
            ],
        ),
        out_shape=[
            jax.ShapeDtypeStruct((TT, W), BF16),
            jax.ShapeDtypeStruct((TT, W), BF16),
            jax.ShapeDtypeStruct((2, TT, width), F32),
            jax.ShapeDtypeStruct((2, TT, width), BF16),
            jax.ShapeDtypeStruct((2, TT, width), BF16),
            jax.ShapeDtypeStruct((4, 4 * HEADS + 8, 8, HEAD), F32),
            jax.ShapeDtypeStruct((4, 4 * HEADS + 8, 8, HEAD), F32),
            jax.ShapeDtypeStruct((8, HEAD), F32),
        ],
        input_output_aliases=aliases,
        compiler_params=pltpu.CompilerParams(vmem_limit_bytes=60 * 2**20),
        cost_estimate=pl.CostEstimate(flops=24 * HEAD * size, bytes_accessed=18 * TT * width, transcendentals=size),
    )(flags, *args)


def finish_kernel(k_ref, own_ref, a_ref, b_ref, kg_ref, *rest):
    gk_ref, gv_ref = rest[-2:]
    for n in range(2):
        cols = slice(n * HEAD, (n + 1) * HEAD)
        k, inv, hat, _ = normed(k_ref[:, cols], kg_ref[...])
        dk, dv = [own_ref[i, :, cols] + a_ref[i, :, cols].astype(F32) + b_ref[i, :, cols].astype(F32) for i in range(2)]
        u = dk * kg_ref[...]
        gk_ref[:, cols] = (inv * u - hat * (inv * inv) * jnp.mean(u * k, -1, keepdims=True)).astype(BF16)
        gv_ref[:, cols] = dv.astype(BF16)


def finish(chunk, k, own, a, b, kg, before):
    base, end = SPLIT[chunk]
    heads = end - base
    wide = pl.BlockSpec((TT, 2 * HEAD), lambda h: (0, h + base // 2))
    pair = pl.BlockSpec((2, TT, 2 * HEAD), lambda h: (0, 0, h))
    in_specs = [wide, pair, pair, pair, pl.BlockSpec((1, HEAD), lambda h: (0, 0))]
    args = [k, own, a, b, kg]
    aliases = {}
    if before is not None:
        aliases = {len(args): 0, len(args) + 1: 1}
        in_specs += [pl.BlockSpec(memory_space=pl.ANY)] * 2
        args += list(before)
    return pl.pallas_call(
        finish_kernel,
        grid=(heads // 2,),
        in_specs=in_specs,
        out_specs=[wide, wide],
        out_shape=[jax.ShapeDtypeStruct((TT, W), BF16)] * 2,
        input_output_aliases=aliases,
        compiler_params=pltpu.CompilerParams(vmem_limit_bytes=60 * 2**20),
        cost_estimate=pl.CostEstimate(flops=20 * TT * heads * HEAD, bytes_accessed=26 * TT * heads * HEAD, transcendentals=TT),
    )(*args)


def send(x, pairs):
    return lax.ppermute(x, "tile", pairs)


INNER = [(i, i ^ 1) for i in range(64)]
OUTER = [(i, (i - 1 ^ 1) + 1) for i in range(1, 63)]


def after(x, *others):
    for other in others:
        zero = jnp.minimum(jnp.abs(other[(-1,) * other.ndim]), 0).astype(x.dtype)
        x = x + zero
    return x


def gather_all(x, packs):
    x = x[None]
    got = send(x, steps_along(0, 1))
    pack = after(packs[0], got)
    inners, outers = [send(pack, INNER)], [send(pack, OUTER)]
    x = jnp.concatenate([x, got], 0)
    stage = [send(x, steps_along(1, by)) for by in range(1, 4)]
    x = jnp.stack([x] + stage)
    stage = [send(x, steps_along(2, by)) for by in range(1, 4)]
    x = jnp.stack([x] + stage)
    pack = after(packs[1], *stage)
    inners.append(send(pack, INNER))
    outers.append(send(pack, OUTER))
    x = x.transpose(3, 1, 0, 2, 4).reshape(4 * HEADS, 32, HEAD)
    return (x, send(x, steps_along(3, 1))), inners, outers


def reduce_text(mine, other, first, second):
    total = mine + send(other.astype(BF16), steps_along(3, -1)).astype(F32)
    for dim in (1, 2, 0):
        if dim == 1:
            parts = [total[i] for i in range(4)]
        else:
            total = after(total, *(list(first) + list(second[:1]) if dim == 2 else second[1:]))
            n = total.shape[1] // SIZES[dim]
            parts = [total[:, i * n : (i + 1) * n] for i in range(SIZES[dim])]
        kind = BF16 if dim == 1 else F32
        got = [send(parts[by].astype(kind), steps_along(dim, -by)).astype(F32) for by in range(1, SIZES[dim])]
        total = functools.reduce(jnp.add, got, parts[0])
    return total[:, 0]


def per_device(query, key, value, text_key, text_value, text_len, window, query_gain, key_gain, grad_out):
    me = lax.axis_index("tile")
    q, k, v, g = query[0], key[0], value[0], grad_out[0]
    bits = lax.dynamic_index_in_dim(window[0], me, 0, keepdims=False)
    below, above = (bits[0] > 0) & (me > 0), (bits[1] > 0) & (me < 63)
    even = me % 2 == 0
    flags = jnp.stack([jnp.where(even, above, below), jnp.where(even, below, above)]).astype(jnp.int32)
    qg, kg = query_gain.reshape(1, HEAD), key_gain.reshape(1, HEAD)

    rows = jnp.stack([text_key[0], text_value[0]]).reshape(2, 2, HEADS, HEAD).transpose(2, 0, 1, 3).reshape(4 * HEADS, HEAD)
    packs = [jnp.stack([k[:, a * HEAD : b * HEAD], v[:, a * HEAD : b * HEAD]]) for a, b in SPLIT]
    texts, inners, outers = gather_all(rows, packs)
    slot = jnp.arange(64)
    here = (me // 32, me // 8 % 4, me // 2 % 4, me % 2)
    back = (slot % 2, slot // 8 % 4, slot // 2 % 4, slot // 32)
    owner = place_of(*[(m - b) % s for m, b, s in zip(here, back, SIZES)])
    index = (owner[None, :] * 2 + jnp.arange(2)[:, None]).reshape(TXT, 1)
    keep = (index < text_len[0]).astype(F32)

    outs, parts = None, []
    for c in range(len(SPLIT)):
        outs = attend(c, flags, q, k, v, g, inners[c], outers[c], texts, keep, qg, kg, outs)
        own, din, dout = outs[2:5]
        parts.append((own, send(din, INNER), send(dout, OUTER)))
    fins = finish(0, k, *parts[0], kg, None)
    summed = reduce_text(outs[5], outs[6], [fins[1][:1, :1]], parts[1][1:])
    fins = finish(1, k, *parts[1], kg, fins)

    gains = summed[4 * HEADS : 4 * HEADS + 2]
    total = gains
    for by in range(1, 4):
        total = total + lax.ppermute(gains, "dp", [(i, (i + by) % 4) for i in range(4)])
    dtn, dtv = [summed[: 4 * HEADS].reshape(HEADS, 2, 2, HEAD)[:, i].transpose(1, 0, 2) for i in range(2)]
    t = text_key[0].astype(F32).reshape(2, HEADS, HEAD)
    inv = lax.rsqrt(jnp.mean(t * t, -1, keepdims=True) + 1e-06)
    u = dtn * key_gain
    gtk = (inv * u - t * inv**3 * jnp.mean(u * t, -1, keepdims=True)).reshape(1, 2, W)
    return (
        outs[0][None],
        outs[1][None],
        fins[0][None],
        fins[1][None],
        gtk,
        dtv.reshape(1, 2, W),
        total[0],
        total[1],
    )


def solution(mesh):
    row = P("dp", "tile", None)
    in_specs = (row, row, row, row, row, P("dp"), P("dp", None, None), P(), P(), row)
    out_specs = (row, row, row, row, row, row, P(), P())
    return jax.shard_map(per_device, mesh=mesh, in_specs=in_specs, out_specs=out_specs, check_vma=False)
```
